256 devices in a mesh: row: 16 (over y, z_hi), col: 16 (over z_lo, x, core).
Axes of the slice: x: 4, y: 4, z: 8 (z_hi: 4, z_lo: 2; z = z_hi * 2 + z_lo), core: 2. Of those that a mesh axis runs over, the one named last changes fastest.
Arguments:
- assembled: float32 [16384, 16384], P('row', 'col'), may hold values from -16 to 1024, as said below
- row_order: int32 [16384], replicated, may hold values from 0 to 16383, as said below
- tile_mask: int32 [64, 64], replicated, may hold values from 0 to 1, as said below
Outputs:
- factored: float32 [16384, 16384], P('row', 'col')
The draws below stay inside these ranges and needn't reach their ends.
Inputs may be any that keep to these rules, and one draw needn't show every extreme that they name: `row_order`: A permutation; each aligned block of 1024 entries holds exactly 64 values from each aligned block of 1024 values. `tile_mask`: Symmetric; every diagonal tile is 1; in every tile row, each aligned group of 4 tiles holds at most 2 filled tiles, and tile row 0 holds exactly 2 in every group. `assembled`: once its rows are put in front order and masked, the front is symmetric and its leading 512 x 512 block is positive definite.
All inputs are finite; a program needn't handle non-finite values.
Results may differ from the reference program's by a relative error of at most 0.0003.
Values sent between devices are 32-bit elements; how exact they have to be, the bound alone decides.
A program may use at most 128 MiB of HBM per device.

```python
import jax
import jax.numpy as jnp
from jax import lax

TB = 256
PW = 512
ROWS_DEV = 1024
ORDER = 16384
TILES = 64
COL_TILES = 4
N_ROW = 16


def balanced_order(key):
    first_key, second_key = jax.random.split(jax.random.fold_in(key, 11))
    share = ROWS_DEV // N_ROW
    source_perm = jax.vmap(lambda k: jax.random.permutation(k, ROWS_DEV))(jax.random.split(first_key, N_ROW)).astype(jnp.int32)
    target_perm = jax.vmap(lambda k: jax.random.permutation(k, ROWS_DEV))(jax.random.split(second_key, N_ROW)).astype(jnp.int32)
    blocks = jnp.arange(N_ROW, dtype=jnp.int32)
    values = blocks[None, :, None] * ROWS_DEV + jnp.transpose(source_perm.reshape(N_ROW, N_ROW, share), (1, 0, 2))
    values = values.reshape(N_ROW, ROWS_DEV)

    def place(slots, entries):
        return jnp.zeros((ROWS_DEV,), jnp.int32).at[slots].set(entries)
    return jax.vmap(place)(target_perm, values).reshape(ORDER)


def draw_row_order(key, part):
    return balanced_order(key)


def draw_assembled(key, part):
    row_order = balanced_order(key)
    key = jax.random.fold_in(key, 5)
    first_key, second_key = jax.random.split(key)
    base = jax.random.uniform(first_key, (ORDER, ORDER), jnp.float32, -1.0, 1.0)
    front = 0.5 * (base + base.T)
    every_row = jnp.arange(ORDER, dtype=jnp.int32)
    in_panel = every_row < PW
    cross = in_panel[:, None] != in_panel[None, :]
    front = jnp.where(cross, 16.0 * front, front)
    spread = jax.random.uniform(second_key, (ORDER,), jnp.float32, 0.0, 1.0)
    diagonal = jnp.where(in_panel, PW + PW * spread, 32.0 + 16.0 * spread)
    front = jnp.where(every_row[:, None] == every_row[None, :], diagonal[:, None], front)
    return jnp.zeros_like(front).at[row_order].set(front)


def draw_tile_mask(key, part):
    key = jax.random.fold_in(key, 7)
    first_key, second_key, third_key = jax.random.split(key, 3)
    groups = TILES // COL_TILES
    colors = jax.vmap(lambda k: jax.random.permutation(k, COL_TILES))(jax.random.split(first_key, groups)).reshape(TILES).astype(jnp.int32)
    relative = (colors - colors[0]) % COL_TILES
    shades = jnp.arange(COL_TILES, dtype=jnp.int32)
    order_rest = 1 + jax.random.permutation(second_key, COL_TILES - 1).astype(jnp.int32)
    listing = jnp.concatenate([jnp.zeros((1,), jnp.int32), order_rest])
    position = jnp.zeros((COL_TILES,), jnp.int32).at[listing].set(shades)
    partner_pos = jnp.where(position % 2 == 0, position + 1, position - 1)
    partner_pos = jnp.where(partner_pos >= COL_TILES, position, partner_pos)
    partner = jnp.take(listing, partner_pos)
    index = jnp.arange(TILES, dtype=jnp.int32)
    bits = jax.random.randint(third_key, (TILES, TILES), 0, 2)
    bits = jnp.where(index[:, None] < index[None, :], bits, bits.T)
    bits = jnp.where((index[:, None] == 0) | (index[None, :] == 0), 1, bits)
    same = relative[:, None] == relative[None, :]
    paired = (jnp.take(partner, relative)[:, None] == relative[None, :]) & (bits == 1)
    return (same | paired).astype(jnp.int32)


def setup_inputs(seed: int = 0) -> dict:
    splits = jax.random.split(jax.random.key(seed), 4)
    return {
        "assembled": draw_assembled(jax.random.fold_in(splits[3], 71), 0),
        "row_order": draw_row_order(jax.random.fold_in(splits[3], 71), 0),
        "tile_mask": draw_tile_mask(jax.random.fold_in(splits[3], 71), 0),
    }


def reference(assembled, row_order, tile_mask):
    gains = tile_mask.astype(jnp.float32)
    panel_gain = jnp.repeat(jnp.repeat(gains[:, :PW // TB], TB, axis=0), TB, axis=1)
    panel = jnp.take(assembled[:, :PW], row_order, axis=0) * panel_gain
    diag_factor = jnp.linalg.cholesky(panel[:PW])
    solved = lax.linalg.triangular_solve(diag_factor, panel, left_side=False, lower=True, transpose_a=True)
    every_row = jnp.arange(ORDER, dtype=jnp.int32)
    padded = jnp.pad(diag_factor, ((0, ORDER - PW), (0, 0)))
    factor_cols = jnp.where(every_row[:, None] < PW, padded, solved)

    def one_block(tile):
        sources = lax.dynamic_slice_in_dim(row_order, tile * TB, TB)
        rows = jnp.take(assembled, sources, axis=0)
        row_gain = jnp.repeat(lax.dynamic_index_in_dim(gains, tile, 0, keepdims=False), TB)
        rows = rows * row_gain[None, :]
        block_cols = lax.dynamic_slice_in_dim(factor_cols, tile * TB, TB)
        update = jnp.dot(block_cols.astype(jnp.float32), factor_cols.T.astype(jnp.float32), precision=lax.Precision.HIGHEST, preferred_element_type=jnp.float32)
        trailing = (rows - update) * row_gain[None, :]
        grow = tile * TB + jnp.arange(TB, dtype=jnp.int32)
        wide_cols = jnp.pad(block_cols, ((0, 0), (0, ORDER - PW)))
        inner = jnp.where(grow[:, None] < PW, jnp.zeros_like(trailing), trailing)
        return jnp.where(every_row[None, :] < PW, wide_cols, inner)
    blocks = lax.map(one_block, jnp.arange(TILES, dtype=jnp.int32))
    return blocks.reshape(ORDER, ORDER)
```

```python
import jax
import jax.numpy as jnp
from jax import lax
from jax.experimental import pallas as pl
from jax.experimental.pallas import tpu as pltpu
from jax.sharding import PartitionSpec as P

F32 = jnp.float32
BF16 = jnp.bfloat16
MESH = pl.DeviceIdType.MESH
NB = 128
GROUP = 4


def bdot(a, b, ca=1, cb=0):
    return lax.dot_general(a, b, (((ca,), (cb,)), ((), ())), preferred_element_type=F32)


def split(value):
    hi = value.astype(BF16)
    return hi, (value - hi.astype(F32)).astype(BF16)


def dot3(a, b, ca=1, cb=0):
    (ah, al), (bh, bl) = a, b
    return bdot(ah, bh, ca, cb) + (bdot(ah, bl, ca, cb) + bdot(al, bh, ca, cb))


def hdot(a, b, ca=1, cb=0):
    return lax.dot_general(
        a, b, (((ca,), (cb,)), ((), ())), precision=lax.Precision.HIGHEST, preferred_element_type=F32
    )


def iota(shape, dim):
    return lax.broadcasted_iota(jnp.int32, shape, dim)


def prefix_counts(flags):
    g, n = flags.shape
    parts = n // 128
    flags = flags.astype(BF16)
    stacked = jnp.concatenate([flags[:, 128 * i : 128 * i + 128] for i in range(parts)], axis=0)
    before = (iota((128, 128), 0) < iota((128, 128), 1)).astype(F32).astype(BF16)
    inner = bdot(stacked, before)
    totals = jnp.sum(stacked.astype(F32), axis=1, keepdims=True)
    out = []
    offset = jnp.zeros((g, 1), F32)
    for i in range(parts):
        out.append(inner[g * i : g * i + g] + offset)
        offset = offset + totals[g * i : g * i + g]
    return jnp.concatenate(out, axis=1)


def unpack_matrix(order_row, n_row, share, rows):
    n = order_row.shape[1]
    source = order_row // n
    flags = (jnp.broadcast_to(source, (n_row, n)) == iota((n_row, n), 0)).astype(F32)
    rank = jnp.sum(flags * prefix_counts(flags), axis=0, keepdims=True)
    slot = source.astype(F32) * share + rank
    column = jnp.transpose(jnp.broadcast_to(slot, (128, n)))[:rows, 0:1]
    want = column.astype(jnp.int32)
    return (want == iota((rows, n_row * share), 1)).astype(F32).astype(BF16)


def expand_tile(pair, first, second):
    half = pair.shape[1] // 2
    return first * pair[:, :half] + second * pair[:, half:]


def reciprocal(d):
    guess = pltpu.reciprocal(d, approx=True)
    guess = guess * (2.0 - d * guess)
    return guess * (2.0 - d * guess)


def tree_sum(terms):
    while len(terms) > 1:
        terms = [terms[i] + terms[i + 1] for i in range(0, len(terms), 2)]
    return terms[0]


def inverse_factor_block(block):
    n = block.shape[0]
    groups = n // 8
    rows = [block[8 * g : 8 * g + 8, :] for g in range(groups)]
    lane = iota((8, n), 1)
    sub = iota((8, n), 0)
    other = [jnp.where(lane == sub + 8 * g, 1.0, 0.0) for g in range(groups)]
    out = []
    for g0 in range(groups):
        lead = rows[g0]
        c0 = 8 * g0

        def replicated(i, j):
            column = jnp.broadcast_to(lead[:, c0 + j : c0 + j + 1], (8, n))
            return jnp.broadcast_to(column[i : i + 1, :], (8, n))

        a = [[replicated(i, j) for j in range(i + 1)] for i in range(8)]
        m = [[None] * 8 for _ in range(8)]
        inv = []
        for k in range(8):
            inv.append(reciprocal(a[k][k]))
            for i in range(k + 1, 8):
                ratio = a[i][k] * inv[k]
                for j in range(k + 1, i + 1):
                    a[i][j] = a[i][j] - ratio * a[j][k]
                for j in range(k):
                    m[i][j] = m[i][j] - ratio * m[k][j]
                m[i][k] = -ratio

        def lower(v):
            res = []
            for i in range(8):
                total = v[i]
                for j in range(i):
                    total = total + m[i][j] * v[j]
                res.append(total)
            return res

        def upper(v):
            v = [v[i] * inv[i] for i in range(8)]
            res = []
            for j in range(8):
                total = v[j]
                for i in range(j + 1, 8):
                    total = total + m[i][j] * v[i]
                res.append(total)
            return res

        own = lower([jnp.broadcast_to(other[g0][i : i + 1, :], (8, n)) for i in range(8)])
        done = own[0] * lax.rsqrt(a[0][0])
        for i in range(1, 8):
            done = jnp.where(sub == i, own[i] * lax.rsqrt(a[i][i]), done)
        out.append(done)
        if g0 == groups - 1:
            break
        t = upper(lower([jnp.broadcast_to(lead[i : i + 1, :], (8, n)) for i in range(8)]))
        u = upper(own)
        for g in range(g0 + 1, groups):
            c = [jnp.broadcast_to(rows[g][:, c0 + j : c0 + j + 1], (8, n)) for j in range(8)]
            rows[g] = rows[g] - tree_sum([c[j] * t[j] for j in range(8)])
            other[g] = other[g] - tree_sum([c[j] * u[j] for j in range(8)])
    return jnp.concatenate(out, axis=0)


def inverse_factor(s_ref, o_ref, a_ref):
    n = s_ref.shape[0]
    a_ref[...] = s_ref[...]
    o_ref[...] = jnp.zeros_like(o_ref)
    for lo in range(0, n, NB):
        hi = lo + NB
        inverse = inverse_factor_block(a_ref[lo:hi, lo:hi])
        if lo > 0:
            o_ref[lo:hi, 0:lo] = hdot(inverse, o_ref[lo:hi, 0:lo])
        o_ref[lo:hi, lo:hi] = inverse
        if hi < n:
            below = hdot(a_ref[hi:, lo:hi], inverse, 1, 1)
            a_ref[hi:, hi:] = a_ref[hi:, hi:] - hdot(below, below, 1, 1)
            o_ref[hi:, 0:hi] = o_ref[hi:, 0:hi] - hdot(below, o_ref[lo:hi, 0:hi])


def exchange_kernel(
    dims, order_ref, sel_ref, x_ref, r_ref, t_ref, s_ref, tr_ref,
    packed, lead, high, low, s_own, rank_ref,
    a2a_send, a2a_recv, z_send, z_recv, y_send, y_recv, b_send, b_recv,
):
    ny, nz, nzl, nx = dims
    n_row, share, half = packed.shape
    n = x_ref.shape[0]
    tile = half // 2
    pw = t_ref.shape[0]
    r = lax.axis_index("row")
    c = lax.axis_index("col")
    n_col = lax.axis_size("col")
    y, z = r // nz, r % nz
    zl, x, core = c // (2 * nx), (c // 2) % nx, c % 2

    barrier = pltpu.get_barrier_semaphore()
    for k in range(1, n_row):
        pl.semaphore_signal(barrier, inc=1, device_id=((r + k) % n_row, c), device_id_type=MESH)
    for k in range(1, n_col):
        pl.semaphore_signal(barrier, inc=1, device_id=(r, (c + k) % n_col), device_id_type=MESH)

    match = order_ref[...] // n == r
    rank_ref[...] = jnp.where(match, prefix_counts(match.astype(F32)), -1.0)
    code_row = (order_ref[...] % n + n * (iota((n_row, n), 1) // tile)).astype(F32)
    high[...], low[...] = split(x_ref[...])

    def pack(group):
        cols = []
        for t in range(GROUP * group, GROUP * group + GROUP):
            hit = jnp.broadcast_to(rank_ref[t : t + 1, :], (share, n)) == iota((share, n), 0).astype(F32)
            code = jnp.where(hit, jnp.broadcast_to(code_row[t : t + 1, :], (share, n)), 0.0)
            cols.append(jnp.sum(code, axis=1, keepdims=True) + float(4 * n * t))
        code = jnp.concatenate(cols, axis=0).astype(jnp.int32)
        rows = GROUP * share
        pick = (code % n == iota((rows, n), 1)).astype(F32).astype(BF16)
        tile_row = (code // n == iota((rows, 128), 1)).astype(F32).astype(BF16)
        weights = bdot(tile_row, sel_ref[...].astype(BF16))
        got = bdot(pick, high[...]) + bdot(pick, low[...])
        for h in range(2):
            total = jnp.zeros((rows, tile), F32)
            for q in range(4):
                w = weights[:, 4 * h + q : 4 * h + q + 1]
                total = total + w * got[:, tile * q : tile * q + tile]
            for i in range(GROUP):
                packed[GROUP * group + i, :, tile * h : tile * h + tile] = total[share * i : share * i + share]

    pack(0)
    lead[r] = packed[0]
    pl.semaphore_wait(barrier, n_row - 1 + n_col - 1)

    def z_copy(k):
        return pltpu.make_async_remote_copy(
            lead.at[r], lead.at[r], z_send.at[k], z_recv.at[k],
            device_id=(y * nz + (z + k) % nz, c), device_id_type=MESH)

    def z_arrival(k):
        slot = lead.at[y * nz + (z - k + nz) % nz]
        return pltpu.make_async_remote_copy(
            slot, slot, z_send.at[k], z_recv.at[k], device_id=(r, c), device_id_type=MESH)

    def y_copy(k, d):
        slot = lead.at[y * nz + (z - k + nz) % nz]
        return pltpu.make_async_remote_copy(
            slot, slot, y_send.at[k * ny + d], y_recv.at[k * ny + d],
            device_id=(((y + d) % ny) * nz + z, c), device_id_type=MESH)

    def y_arrival(k, d):
        slot = lead.at[((y - d + ny) % ny) * nz + (z - k + nz) % nz]
        return pltpu.make_async_remote_copy(
            slot, slot, y_send.at[k * ny + d], y_recv.at[k * ny + d], device_id=(r, c), device_id_type=MESH)

    for k in range(1, nz):
        z_copy(k).start()
    for d in range(1, ny):
        y_copy(0, d).start()
    for group in range(1, n_row // GROUP):
        pack(group)
    for k in range(1, nz):
        z_arrival(k).wait_recv()
        for d in range(1, ny):
            y_copy(k, d).start()

    def a2a_copy(k):
        target = (r + k) % n_row
        return pltpu.make_async_remote_copy(
            packed.at[target], r_ref.at[r], a2a_send.at[k], a2a_recv.at[k],
            device_id=(target, c), device_id_type=MESH)

    def a2a_arrival(k):
        slot = r_ref.at[(r - k + n_row) % n_row]
        return pltpu.make_async_remote_copy(
            slot, slot, a2a_send.at[k], a2a_recv.at[k], device_id=(r, c), device_id_type=MESH)

    for k in range(1, n_row):
        @pl.when((r + k) % n_row != 0)
        def _():
            a2a_copy(k).start()

    r_ref[r] = packed[r]
    for k in range(nz):
        for d in range(1, ny):
            y_arrival(k, d).wait_recv()

    unpack = unpack_matrix(order_ref[0:1, :], n_row, share, pw)
    lead_high, lead_low = split(lead[...].reshape(n_row * share, half))
    t_ref[...] = bdot(unpack, lead_high) + bdot(unpack, lead_low)

    @pl.when(c == 0)
    def _():
        for a in range(2):
            pair = t_ref[tile * a : tile * a + tile, :]
            for q in range(2):
                s_own[tile * a : tile * a + tile, tile * q : tile * q + tile] = expand_tile(
                    pair, sel_ref[a : a + 1, q : q + 1], sel_ref[a : a + 1, 4 + q : 5 + q])

    quarter = pw // nx

    class Broadcast:
        def __init__(self, index, own, dst, src):
            self.own, self.dst = own, dst
            self.sems = index * 16
            self.zs, self.xs, self.cs = src // (2 * nx), (src // 2) % nx, src % 2
            self.is_src = c == src
            self.on_core = core == self.cs
            self.on_zs = zl == self.zs

        def copy(self, ref, part, sem, target):
            rows = pl.ds(pl.multiple_of(part * quarter, quarter), quarter)
            return pltpu.make_async_remote_copy(
                ref.at[rows], self.dst.at[rows], b_send.at[self.sems + sem], b_recv.at[self.sems + sem],
                device_id=(r, target), device_id_type=MESH)

        def at(self, z_, x_, core_):
            return z_ * (2 * nx) + x_ * 2 + core_

        def first(self, dx):
            part = (self.xs + dx) % nx
            return self.copy(self.own, part, dx, self.at(self.zs, part, self.cs))

        def stage1(self):
            @pl.when(self.is_src)
            def _():
                for dx in range(1, nx):
                    self.first(dx).start()
                rows = pl.ds(pl.multiple_of(self.xs * quarter, quarter), quarter)
                self.dst[rows, :] = self.own[rows, :]

        def stage2(self):
            @pl.when(self.on_core & self.on_zs)
            def _():
                @pl.when(x != self.xs)
                def _():
                    self.copy(self.dst, x, (x - self.xs + nx) % nx, c).wait_recv()
                self.copy(self.dst, x, 4, self.at(1 - zl, x, core)).start()

        def stage3(self):
            @pl.when(self.on_core)
            def _():
                @pl.when(jnp.logical_not(self.on_zs))
                def _():
                    self.copy(self.dst, x, 4, c).wait_recv()
                for dx in range(1, nx):
                    self.copy(self.dst, x, 4 + dx, self.at(zl, (x + dx) % nx, core)).start()
                self.copy(self.dst, x, 8, self.at(zl, x, 1 - core)).start()

        def stage4(self):
            @pl.when(self.on_core)
            def _():
                for dx in range(1, nx):
                    part = (x - dx + nx) % nx
                    self.copy(self.dst, part, 4 + dx, c).wait_recv()
                    self.copy(self.dst, part, 8 + dx, self.at(zl, x, 1 - core)).start()

            @pl.when(jnp.logical_not(self.on_core))
            def _():
                for dx in range(nx):
                    self.copy(self.dst, (x - dx + nx) % nx, 8 + dx, c).wait_recv()

        def finish(self):
            @pl.when(self.is_src)
            def _():
                for dx in range(1, nx):
                    self.first(dx).wait_send()

            @pl.when(self.on_core)
            def _():
                @pl.when(self.on_zs)
                def _():
                    self.copy(self.dst, x, 4, c).wait_send()
                for dx in range(1, nx):
                    self.copy(self.dst, x, 4 + dx, c).wait_send()
                for dx in range(nx):
                    self.copy(self.dst, (x - dx + nx) % nx, 8 + dx, c).wait_send()

    both = [Broadcast(0, s_own, s_ref, 0), Broadcast(1, t_ref, tr_ref, r)]
    for step in ("stage1", "stage2", "stage3", "stage4", "finish"):
        for b in both:
            getattr(b, step)()

    for k in range(1, nz):
        z_copy(k).wait_send()
    for k in range(nz):
        for d in range(1, ny):
            y_copy(k, d).wait_send()
    for k in range(1, n_row):
        @pl.when((r + k) % n_row != 0)
        def _():
            a2a_copy(k).wait_send()

    @pl.when(r != 0)
    def _():
        for k in range(1, n_row):
            a2a_arrival(k).wait_recv()

    @pl.when(r == 0)
    def _():
        r_ref[...] = lead[...]


def exchange(order, sel, block, n_row, n_col):
    n = block.shape[0]
    share, half, pw = n // n_row, n // 2, n // 2
    dims = (n_row // 4, 4, 2, n_col // 4)
    vmem = pl.BlockSpec(memory_space=pltpu.VMEM)
    dma = pltpu.SemaphoreType.DMA

    def kernel(*refs):
        exchange_kernel(dims, *refs)

    return pl.pallas_call(
        kernel,
        out_shape=[
            jax.ShapeDtypeStruct((n_row, share, half), F32),
            jax.ShapeDtypeStruct((pw, half), F32),
            jax.ShapeDtypeStruct((pw, pw), F32),
            jax.ShapeDtypeStruct((pw, half), F32),
        ],
        in_specs=[vmem] * 3,
        out_specs=[vmem] * 4,
        scratch_shapes=[
            pltpu.VMEM((n_row, share, half), F32),
            pltpu.VMEM((n_row, share, half), F32),
            pltpu.VMEM((n, n), BF16),
            pltpu.VMEM((n, n), BF16),
            pltpu.VMEM((pw, pw), F32),
            pltpu.VMEM((n_row, n), F32),
            dma((n_row,)), dma((n_row,)),
            dma((4,)), dma((4,)),
            dma((n_row,)), dma((n_row,)),
            dma((32,)), dma((32,)),
        ],
        compiler_params=pltpu.CompilerParams(
            collective_id=0, has_side_effects=True, vmem_limit_bytes=52 * 2**20
        ),
        name="exchange",
    )(order, sel, block)


def factor(leading):
    n = leading.shape[0]
    vmem = pl.BlockSpec(memory_space=pltpu.VMEM)
    return pl.pallas_call(
        inverse_factor,
        out_shape=jax.ShapeDtypeStruct((n, n), F32),
        in_specs=[vmem],
        out_specs=vmem,
        scratch_shapes=[pltpu.VMEM((n, n), F32)],
        compiler_params=pltpu.CompilerParams(vmem_limit_bytes=32 * 2**20),
        name="factor",
    )(leading)


def update_kernel(
    n_row, here_ref, order_ref, sel_ref, lead_sel_ref, r_ref, t_ref, tr_ref, inv_ref, o_ref,
    r_high, r_low, x_high, x_low, z_high, z_low, x_own, unpack_ref,
):
    a = pl.program_id(0)
    n = o_ref.shape[1]
    tile = n // 4
    share = n // n_row
    r = here_ref[0]
    c = here_ref[1]

    @pl.when(a == 0)
    def _():
        unpack_ref[...] = unpack_matrix(order_ref[...], n_row, share, n)
        r_high[...], r_low[...] = split(r_ref[...])
        inv = split(inv_ref[...])

        def dense(ref, base):
            rows = []
            for i in range(2):
                pair = ref[tile * i : tile * i + tile, :]
                rows.append(jnp.concatenate([
                    expand_tile(
                        pair,
                        lead_sel_ref[i : i + 1, base + q : base + q + 1],
                        lead_sel_ref[i : i + 1, base + 4 + q : base + 5 + q],
                    ) for q in range(4)], axis=1))
            return jnp.concatenate(rows, axis=0)

        own = dot3(split(jnp.transpose(dense(tr_ref, 8))), inv, 1, 1)
        x_own[...] = own
        x_high[...], x_low[...] = split(own)
        z_high[...], z_low[...] = split(dot3(inv, split(dense(t_ref, 0))))

    rows = pl.ds(pl.multiple_of(a * tile, tile), tile)
    one_hot = unpack_ref[rows, :]
    pair = bdot(one_hot, r_high[...]) + bdot(one_hot, r_low[...])
    panel = (x_high[rows, :], x_low[rows, :])
    sel = sel_ref[pl.ds(a, 1), :]
    live = jnp.where((r == 0) & (a < 2), 0.0, 1.0)
    for q in range(4):
        cols = slice(tile * q, tile * q + tile)
        first, second = sel[:, q : q + 1], sel[:, 4 + q : 5 + q]
        change = dot3(panel, (z_high[:, cols], z_low[:, cols]))
        o_ref[:, cols] = (expand_tile(pair, first, second) - (first + second) * change) * live

    @pl.when(c == 0)
    def _():
        mine = x_own[rows, :]
        above = iota(mine.shape, 1) > iota(mine.shape, 0) + a * tile
        o_ref[:, : 2 * tile] = jnp.where(above & (r == 0) & (a < 2), 0.0, mine)


def update(here, order, sel, lead_sel, arrived, top, top_r, inverse, n_row):
    n = order.shape[1]
    tile, pw = n // 4, n // 2

    def whole(shape):
        return pl.BlockSpec(shape, lambda a: (0,) * len(shape))

    def kernel(*refs):
        update_kernel(n_row, *refs)

    return pl.pallas_call(
        kernel,
        out_shape=jax.ShapeDtypeStruct((n, n), F32),
        grid=(4,),
        in_specs=[
            pl.BlockSpec(memory_space=pltpu.SMEM),
            whole((1, n)), whole((8, 128)), whole((8, 128)),
            whole((n, pw)), whole((pw, pw)), whole((pw, pw)), whole((pw, pw)),
        ],
        out_specs=pl.BlockSpec((tile, n), lambda a: (a, 0)),
        scratch_shapes=[
            pltpu.VMEM((n, pw), BF16), pltpu.VMEM((n, pw), BF16),
            pltpu.VMEM((n, pw), BF16), pltpu.VMEM((n, pw), BF16),
            pltpu.VMEM((pw, n), BF16), pltpu.VMEM((pw, n), BF16),
            pltpu.VMEM((n, pw), F32), pltpu.VMEM((n, n), BF16),
        ],
        compiler_params=pltpu.CompilerParams(vmem_limit_bytes=52 * 2**20),
        name="update",
    )(here, order, sel, lead_sel, arrived, top, top_r, inverse)


def selections(filled):
    filled = filled.astype(jnp.int32)
    a, b, c, d = (filled[:, i : i + 1] for i in range(4))
    order = jnp.concatenate([a, a + b, a + b + c, a + b + c + d], axis=1)
    return jnp.concatenate([filled * (order == 1), filled * (order == 2)], axis=1).astype(F32)


def on_device(assembled, row_order, tile_mask):
    n = assembled.shape[0]
    n_row, n_col = lax.axis_size("row"), lax.axis_size("col")
    r, c = lax.axis_index("row"), lax.axis_index("col")
    tiles = tile_mask.shape[0]
    order = row_order.reshape(n_row, n)
    sel = selections(lax.dynamic_slice_in_dim(tile_mask, 4 * c, 4, axis=1))
    sel_r = selections(lax.dynamic_slice(tile_mask, (0, 4 * r), (8, 4)))
    sel_pad = jnp.pad(sel, ((0, 128 - tiles), (0, 120)))
    lead_sel = jnp.pad(jnp.concatenate([sel[:8], sel_r], axis=1), ((0, 0), (0, 112)))
    own_sel = jnp.pad(lax.dynamic_slice_in_dim(sel, 4 * r, 4), ((0, 4), (0, 120)))
    arrived, top, leading, top_r = exchange(order, sel_pad, assembled, n_row, n_col)
    inverse = factor(leading)
    here = jnp.stack([r, c]).astype(jnp.int32)
    own_order = lax.dynamic_slice_in_dim(order, r, 1)
    return update(
        here, own_order, own_sel, lead_sel, arrived.reshape(n, n // 2), top, top_r, inverse, n_row
    )


def solution(mesh):
    in_specs = (P("row", "col"), P(), P())
    out_specs = P("row", "col")
    return jax.shard_map(
        on_device, mesh=mesh, in_specs=in_specs, out_specs=out_specs, check_vma=False
    )
```

```python
import jax
import jax.numpy as jnp
from jax import lax
from jax.experimental import pallas as pl
from jax.experimental.pallas import tpu as pltpu
from jax.sharding import PartitionSpec as P

F32 = jnp.float32
BF16 = jnp.bfloat16
MESH = pl.DeviceIdType.MESH
NB = 128


def bdot(a, b, ca=1, cb=0):
    return lax.dot_general(a, b, (((ca,), (cb,)), ((), ())), preferred_element_type=F32)


def split(value):
    hi = value.astype(BF16)
    return hi, (value - hi.astype(F32)).astype(BF16)


def dot3(a, b, ca=1, cb=0):
    (ah, al), (bh, bl) = a, b
    return bdot(ah, bh, ca, cb) + (bdot(ah, bl, ca, cb) + bdot(al, bh, ca, cb))


def hdot(a, b, ca=1, cb=0):
    return lax.dot_general(
        a, b, (((ca,), (cb,)), ((), ())), precision=lax.Precision.HIGHEST, preferred_element_type=F32
    )


def iota(shape, dim):
    return lax.broadcasted_iota(jnp.int32, shape, dim)


def prefix_counts(flags):
    g, n = flags.shape
    parts = n // 128
    flags = flags.astype(BF16)
    stacked = jnp.concatenate([flags[:, 128 * i : 128 * i + 128] for i in range(parts)], axis=0)
    before = (iota((128, 128), 0) < iota((128, 128), 1)).astype(F32).astype(BF16)
    inner = bdot(stacked, before)
    totals = jnp.sum(stacked.astype(F32), axis=1, keepdims=True)
    out = []
    offset = jnp.zeros((g, 1), F32)
    for i in range(parts):
        out.append(inner[g * i : g * i + g] + offset)
        offset = offset + totals[g * i : g * i + g]
    return jnp.concatenate(out, axis=1)


def arrival_slots(order_row, n_row, share):
    n = order_row.shape[1]
    source = order_row // n
    flags = (jnp.broadcast_to(source, (n_row, n)) == iota((n_row, n), 0)).astype(F32)
    rank = jnp.sum(flags * prefix_counts(flags), axis=0, keepdims=True)
    slot = source.astype(F32) * share + rank
    return jnp.transpose(jnp.broadcast_to(slot, (128, n))).astype(jnp.int32)


def one_hot(slots, n):
    return (slots[:, 0:1] == iota((slots.shape[0], n), 1)).astype(F32).astype(BF16)


def selections(mask, group):
    tiles = mask.shape[1]
    at, lane = iota((tiles, 128), 0), iota((tiles, 128), 1)
    start = 4 * group
    here = (at == start + lane % 4) & (lane < 8)
    upto = (at >= start) & (at <= start + lane % 4) & (lane < 8)
    mask = mask.astype(F32).astype(BF16)
    filled = bdot(mask, here.astype(F32).astype(BF16))
    count = bdot(mask, upto.astype(F32).astype(BF16))
    return filled * (count == (1 + lane[:1] // 4).astype(F32)).astype(F32)


def expand_tile(pair, first, second):
    half = pair.shape[1] // 2
    return first * pair[:, :half] + second * pair[:, half:]


def reciprocal(d):
    guess = pltpu.reciprocal(d, approx=True)
    guess = guess * (2.0 - d * guess)
    return guess * (2.0 - d * guess)


def tree_sum(terms):
    while len(terms) > 1:
        terms = [terms[i] + terms[i + 1] for i in range(0, len(terms), 2)]
    return terms[0]


def inverse_factor_block(block):
    n = block.shape[0]
    rows = block
    other = (iota((n, n), 0) == iota((n, n), 1)).astype(F32)
    sub = iota((8, n), 0)
    out = []
    for c0 in range(0, n, 8):
        lead, lead_other = rows[:8], other[:8]

        def replicated(i, j):
            column = jnp.broadcast_to(lead[:, c0 + j : c0 + j + 1], (8, n))
            return jnp.broadcast_to(column[i : i + 1, :], (8, n))

        a = [[replicated(i, j) for j in range(i + 1)] for i in range(8)]
        m = [[None] * 8 for _ in range(8)]
        inv = []
        for k in range(8):
            inv.append(reciprocal(a[k][k]))
            for i in range(k + 1, 8):
                ratio = a[i][k] * inv[k]
                for j in range(k + 1, i + 1):
                    a[i][j] = a[i][j] - ratio * a[j][k]
                for j in range(k):
                    m[i][j] = m[i][j] - ratio * m[k][j]
                m[i][k] = -ratio

        def lower(v):
            res = []
            for i in range(8):
                total = v[i]
                for j in range(i):
                    total = total + m[i][j] * v[j]
                res.append(total)
            return res

        def upper(v):
            v = [v[i] * inv[i] for i in range(8)]
            res = []
            for j in range(8):
                total = v[j]
                for i in range(j + 1, 8):
                    total = total + m[i][j] * v[i]
                res.append(total)
            return res

        own = lower([jnp.broadcast_to(lead_other[i : i + 1, :], (8, n)) for i in range(8)])
        done = own[0] * lax.rsqrt(a[0][0])
        for i in range(1, 8):
            done = jnp.where(sub == i, own[i] * lax.rsqrt(a[i][i]), done)
        out.append(done)
        if c0 + 8 == n:
            break
        t = upper(lower([jnp.broadcast_to(lead[i : i + 1, :], (8, n)) for i in range(8)]))
        u = upper(own)
        rows, other = rows[8:], other[8:]
        left = rows.shape[0]
        c = [jnp.broadcast_to(rows[:, c0 + j : c0 + j + 1], (left, n)) for j in range(8)]

        def combine(v):
            if left == 8:
                return tree_sum([c[j] * v[j] for j in range(8)])
            return tree_sum([c[j] * jnp.broadcast_to(v[j][0:1, :], (left, n)) for j in range(8)])

        rows, other = rows - combine(t), other - combine(u)
    return jnp.concatenate(out, axis=0)


def factor_blocks(s_ref, a_ref, o_ref, done):
    n = s_ref.shape[0]
    a_ref[...] = s_ref[...]
    o_ref[...] = (iota((n, n), 0) == iota((n, n), 1)).astype(F32)

    def step(b, carry):
        start = pl.multiple_of(b * NB, NB)
        block = pl.ds(start, NB)
        inverse = inverse_factor_block(a_ref[block, block])
        mine = hdot(inverse, o_ref[block, :])
        done(b, mine)
        below = hdot(a_ref[:, block], inverse, 1, 1)
        below = jnp.where(iota((n, NB), 0) >= start + NB, below, 0.0)
        a_ref[...] = a_ref[...] - hdot(below, below, 1, 1)
        o_ref[...] = o_ref[...] - hdot(below, mine)
        return carry

    lax.fori_loop(0, n // NB, step, 0)


def exchange_kernel(
    dims, order_ref, mask_ref, x_ref, r_ref, xh_ref, xl_ref, zh_ref, zl_ref,
    packed, lead, lead2, strip, high, low, rank_ref, t_ref, t2_ref, t0_ref, tr_ref, s_ref, a_ref, o_ref, inv_ref,
    a2a_send, a2a_recv, z_send, z_recv, y_send, y_recv, b_send, b_recv, far_send, far_recv,
    strip_send, strip_recv, fill_send, fill_recv, inv_send, inv_recv, go,
):
    ny, nz, nzl, nx = dims
    n_row, share, half = packed.shape
    n = x_ref.shape[0]
    tile = half // 2
    pw = t_ref.shape[0]
    r = lax.axis_index("row")
    c = lax.axis_index("col")
    n_col = lax.axis_size("col")
    y, z = r // nz, r % nz
    plane = 2 * nx
    zl, x, core = c // plane, (c // 2) % nx, c % 2
    width = half // nx

    def flip(col):
        return (col + plane) % n_col

    barrier = pltpu.get_barrier_semaphore()
    for k in range(1, n_row):
        pl.semaphore_signal(barrier, inc=1, device_id=((r + k) % n_row, c), device_id_type=MESH)
    for k in range(1, n_col):
        pl.semaphore_signal(barrier, inc=1, device_id=(r, (c + k) % n_col), device_id_type=MESH)

    @pl.when(c == flip(r))
    def _():
        for k in range(n_row):
            pl.semaphore_signal(barrier, inc=1, device_id=(k, r), device_id_type=MESH)

    match = order_ref[...] // n == r
    rank_ref[...] = jnp.where(match, prefix_counts(match.astype(F32)), -1.0)
    code_row = (order_ref[...] % n + n * (iota((n_row, n), 1) // tile)).astype(F32)
    sel = selections(mask_ref[...], c)
    high[...], low[...] = split(x_ref[...])

    def pack(first, last):
        cols = []
        for t in range(first, last):
            hit = jnp.broadcast_to(rank_ref[t : t + 1, :], (share, n)) == iota((share, n), 0).astype(F32)
            code = jnp.where(hit, jnp.broadcast_to(code_row[t : t + 1, :], (share, n)), 0.0)
            cols.append(jnp.sum(code, axis=1, keepdims=True) + float(4 * n * t))
        code = jnp.concatenate(cols, axis=0).astype(jnp.int32)
        rows = (last - first) * share
        pick = (code % n == iota((rows, n), 1)).astype(F32).astype(BF16)
        tile_row = (code // n == iota((rows, 4 * n_row), 1)).astype(F32).astype(BF16)
        weights = bdot(tile_row, sel.astype(BF16))
        got = bdot(pick, high[...]) + bdot(pick, low[...])
        for h in range(2):
            total = jnp.zeros((rows, tile), F32)
            for q in range(4):
                w = weights[:, 4 * h + q : 4 * h + q + 1]
                total = total + w * got[:, tile * q : tile * q + tile]
            for i in range(last - first):
                packed[first + i, :, tile * h : tile * h + tile] = total[share * i : share * i + share]

    pack(0, 4)
    lead[r] = packed[0]
    pl.semaphore_wait(barrier, n_row - 1 + n_col)

    class Gather:
        def __init__(self, ref, base):
            self.ref, self.base = ref, base

        def copy(self, slot, sends, recvs, sem, row):
            slot = self.ref.at[slot]
            return pltpu.make_async_remote_copy(
                slot, slot, sends.at[self.base + sem], recvs.at[self.base + sem],
                device_id=(row, c), device_id_type=MESH)

        def z_copy(self, k):
            return self.copy(r, z_send, z_recv, k, y * nz + (z + k) % nz)

        def z_arrival(self, k):
            return self.copy(y * nz + (z - k + nz) % nz, z_send, z_recv, k, r)

        def y_copy(self, k, d):
            return self.copy(y * nz + (z - k + nz) % nz, y_send, y_recv, k * ny + d, ((y + d) % ny) * nz + z)

        def y_arrival(self, k, d):
            return self.copy(
                ((y - d + ny) % ny) * nz + (z - k + nz) % nz, y_send, y_recv, k * ny + d, r)

        def start_z(self):
            for k in range(1, nz):
                self.z_copy(k).start()

        def start_y(self):
            for d in range(1, ny):
                self.y_copy(0, d).start()

        def forward(self):
            for k in range(1, nz):
                self.z_arrival(k).wait_recv()
                for d in range(1, ny):
                    self.y_copy(k, d).start()

        def receive(self):
            for k in range(nz):
                for d in range(1, ny):
                    self.y_arrival(k, d).wait_recv()

        def finish(self):
            for k in range(1, nz):
                self.z_copy(k).wait_send()
            for k in range(nz):
                for d in range(1, ny):
                    self.y_copy(k, d).wait_send()

    own_lead = Gather(lead, 0)
    top_strip = Gather(strip, n_row)

    def scatter_copy(p, q):
        return pltpu.make_async_remote_copy(
            packed.at[0, :, pl.ds(q * width, width)], strip.at[r], strip_send.at[p * nx + q], strip_recv.at[0],
            device_id=(r, p * plane + 2 * q), device_id_type=MESH)

    def fill_copy(dx):
        cols = pl.ds(pl.multiple_of(x * width, width), width)
        return pltpu.make_async_remote_copy(
            t0_ref.at[:, cols], t0_ref.at[:, cols], fill_send.at[dx], fill_recv.at[dx],
            device_id=(r, zl * plane + 2 * ((x + dx) % nx)), device_id_type=MESH)

    def fill_arrival(dx):
        cols = pl.ds(pl.multiple_of(((x - dx + nx) % nx) * width, width), width)
        return pltpu.make_async_remote_copy(
            t0_ref.at[:, cols], t0_ref.at[:, cols], fill_send.at[dx], fill_recv.at[dx],
            device_id=(r, c), device_id_type=MESH)

    def inverse_copy(part):
        rows = pl.ds(0, pw - NB) if part == 0 else pl.ds(pw - NB, NB)
        return pltpu.make_async_remote_copy(
            inv_ref.at[rows], inv_ref.at[rows], inv_send.at[part], inv_recv.at[part],
            device_id=(r, c + 1 - 2 * core), device_id_type=MESH)

    def far_copy():
        return pltpu.make_async_remote_copy(
            lead.at[r], lead2.at[r], far_send.at[0], far_recv.at[r], device_id=(c, flip(c)), device_id_type=MESH)

    def far_arrival(k):
        return pltpu.make_async_remote_copy(
            lead2.at[k], lead2.at[k], far_send.at[0], far_recv.at[k], device_id=(r, c), device_id_type=MESH)

    matching = c == flip(r)

    offsets = [(dy, dz) for dy in range(ny) for dz in range(nz) if dy + dz > 0]

    def a2a_copy(dy, dz):
        target = ((y + dy) % ny) * nz + (z + dz) % nz
        return target, pltpu.make_async_remote_copy(
            packed.at[target], r_ref.at[r], a2a_send.at[dy * nz + dz], a2a_recv.at[dy * nz + dz],
            device_id=(target, c), device_id_type=MESH)

    def a2a_arrival(dy, dz):
        slot = r_ref.at[((y - dy + ny) % ny) * nz + (z - dz + nz) % nz]
        return pltpu.make_async_remote_copy(
            slot, slot, a2a_send.at[dy * nz + dz], a2a_recv.at[dy * nz + dz], device_id=(r, c), device_id_type=MESH)

    def start_a2a(dy):
        for dz in range(nz):
            if dy + dz > 0:
                target, copy = a2a_copy(dy, dz)
                pl.when(target != 0)(copy.start)

    @pl.when(c == 0)
    def _():
        for p in range(nzl):
            for q in range(nx):
                if p + q > 0:
                    scatter_copy(p, q).start()
        strip[r] = packed[0, :, 0:width]

    own_lead.start_z()
    own_lead.start_y()
    far_copy().start()
    pack(4, n_row)
    r_ref[r] = packed[r]

    @pl.when(core == 0)
    def _():
        @pl.when(c != 0)
        def _():
            scatter_copy(0, 1).wait_recv()
        top_strip.start_z()
        top_strip.start_y()
        top_strip.forward()
        pl.semaphore_signal(go, inc=1, device_id=(r, c + 1), device_id_type=MESH)

    own_lead.forward()

    @pl.when(core == 1)
    def _():
        pl.semaphore_wait(go, 1)

    for dy in range(ny):
        start_a2a(dy)

    def in_order(ref, cols):
        unpack = one_hot(arrival_slots(order_ref[0:1, :], n_row, share)[:pw], n)
        first, second = split(ref[...].reshape(n_row * share, cols))
        return bdot(unpack, first) + bdot(unpack, second)

    class Broadcast:
        def __init__(self, index, src, dst, start, rows):
            self.src, self.dst, self.start, self.rows = src, dst, start, rows
            self.sems = index * 16
            self.xs, self.cs = src // 2, src % 2
            self.part_rows = rows // nx
            self.hub = x == self.xs

        def part(self, p):
            return pl.ds(pl.multiple_of(self.start + p * self.part_rows, self.part_rows), self.part_rows)

        def copy(self, src, dst, sem, target):
            return pltpu.make_async_remote_copy(
                src, dst, b_send.at[self.sems + sem], b_recv.at[self.sems + sem],
                device_id=(r, target), device_id_type=MESH)

        def whole(self, own):
            rows = pl.ds(self.start, self.rows)
            return self.copy(own.at[rows], self.dst.at[rows], 0, c + 1 - 2 * core)

        def piece(self, p, sem, x_, core_):
            rows = self.dst.at[self.part(p)]
            return self.copy(rows, rows, sem, zl * plane + x_ * 2 + core_)

        def lift(self, own):
            @pl.when(core == 1)
            def _():
                self.dst[...] = own[...]

            @pl.when(core == 0)
            def _():
                self.whole(own).start()

        def relay(self):
            @pl.when(self.hub)
            def _():
                @pl.when(self.cs == 0)
                def _():
                    self.whole(self.dst).wait_recv()
                for dx in range(1, nx):
                    p = (x + dx) % nx
                    self.piece(p, dx, p, 1).start()

            @pl.when(jnp.logical_not(self.hub))
            def _():
                self.piece(x, (x - self.xs + nx) % nx, x, 0).wait_recv()
            for dx in range(1, nx):
                @pl.when((x + dx) % nx != self.xs)
                def _():
                    self.piece(x, 4 + dx, (x + dx) % nx, 1).start()
            self.piece(x, 8, x, 0).start()
            for dx in range(1, nx):
                p = (x - dx + nx) % nx

                @pl.when(jnp.logical_not(self.hub))
                def _():
                    self.piece(p, 4 + dx, x, 0).wait_recv()
                self.piece(p, 8 + dx, x, 0).start()

        def receive(self):
            for dx in range(nx):
                self.piece((x - dx + nx) % nx, 8 + dx, x, 1).wait_recv()

        def finish(self):
            @pl.when(c % plane == self.src)
            def _():
                @pl.when(core == 0)
                def _():
                    self.whole(self.dst).wait_send()

            @pl.when(core == 1)
            def _():
                @pl.when(self.hub)
                def _():
                    for dx in range(1, nx):
                        self.piece((x + dx) % nx, dx, x, 0).wait_send()
                for dx in range(1, nx):
                    @pl.when((x + dx) % nx != self.xs)
                    def _():
                        self.piece(x, 4 + dx, x, 0).wait_send()
                for dx in range(nx):
                    self.piece((x - dx + nx) % nx, 8 + dx, x, 0).wait_send()

    panel = Broadcast(0, r % plane, tr_ref, 0, pw)

    def own_top():
        own_lead.receive()
        t_ref[...] = in_order(lead, half)
        pl.when(c == r)(lambda: panel.lift(t_ref))

        @pl.when(matching)
        def _():
            for k in range(n_row):
                far_arrival(k).wait_recv()
            t2_ref[...] = in_order(lead2, half)
            panel.lift(t2_ref)

    @pl.when(core == 0)
    def _():
        top_strip.receive()
        t0_ref[:, pl.ds(pl.multiple_of(x * width, width), width)] = in_order(strip, width)
        for dx in range(1, nx):
            fill_copy(dx).start()
        for dx in range(1, nx):
            fill_arrival(dx).wait_recv()
        marks = selections(mask_ref[...], 0)
        for a in range(2):
            pair = t0_ref[tile * a : tile * a + tile, :]
            for q in range(2):
                s_ref[tile * a : tile * a + tile, tile * q : tile * q + tile] = expand_tile(
                    pair, marks[a : a + 1, q : q + 1], marks[a : a + 1, 4 + q : 5 + q])

        def done(b, rows):
            inv_ref[pl.ds(pl.multiple_of(b * NB, NB), NB), :] = rows
            for part in range(2):
                pl.when(b == pw // NB - 2 + part)(inverse_copy(part).start)
            pl.when(b == pw // NB - 2)(own_top)

        factor_blocks(s_ref, a_ref, o_ref, done)
        panel.receive()

    @pl.when(core == 1)
    def _():
        own_top()
        panel.relay()
        for part in range(2):
            inverse_copy(part).wait_recv()

    def dense(pairs, marks):
        rows = []
        for i in range(2):
            pair = pairs[tile * i : tile * i + tile, :]
            rows.append(jnp.concatenate([
                expand_tile(pair, marks[i : i + 1, q : q + 1], marks[i : i + 1, 4 + q : 5 + q])
                for q in range(4)], axis=1))
        return jnp.concatenate(rows, axis=0)

    inverse = split(inv_ref[...])
    sel_r = selections(mask_ref[...], r)
    zh_ref[...], zl_ref[...] = split(dot3(inverse, split(dense(t_ref[...], sel))))
    xh_ref[...], xl_ref[...] = split(
        dot3(split(jnp.transpose(dense(tr_ref[...], sel_r))), inverse, 1, 1))

    panel.finish()
    own_lead.finish()
    far_copy().wait_send()

    @pl.when(c == 0)
    def _():
        for p in range(nzl):
            for q in range(nx):
                if p + q > 0:
                    scatter_copy(p, q).wait_send()

    @pl.when(core == 0)
    def _():
        top_strip.finish()
        for dx in range(1, nx):
            fill_copy(dx).wait_send()
        for part in range(2):
            inverse_copy(part).wait_send()

    for dy, dz in offsets:
        target, copy = a2a_copy(dy, dz)
        pl.when(target != 0)(copy.wait_send)

    @pl.when(r != 0)
    def _():
        for dy, dz in offsets:
            a2a_arrival(dy, dz).wait_recv()

    @pl.when(r == 0)
    def _():
        r_ref[...] = lead[...]


def exchange(order, mask, block, n_row, n_col):
    n = block.shape[0]
    share, half, pw = n // n_row, n // 2, n // 2
    dims = (n_row // 4, 4, 2, n_col // 4)
    vmem = pl.BlockSpec(memory_space=pltpu.VMEM)
    dma = pltpu.SemaphoreType.DMA
    square = pltpu.VMEM((pw, pw), F32)

    def kernel(*refs):
        exchange_kernel(dims, *refs)

    return pl.pallas_call(
        kernel,
        out_shape=[
            jax.ShapeDtypeStruct((n_row, share, half), F32),
            jax.ShapeDtypeStruct((n, pw), BF16),
            jax.ShapeDtypeStruct((n, pw), BF16),
            jax.ShapeDtypeStruct((pw, n), BF16),
            jax.ShapeDtypeStruct((pw, n), BF16),
        ],
        in_specs=[vmem] * 3,
        out_specs=[vmem] * 5,
        scratch_shapes=[
            pltpu.VMEM((n_row, share, half), F32),
            pltpu.VMEM((n_row, share, half), F32),
            pltpu.VMEM((n_row, share, half), F32),
            pltpu.VMEM((n_row, share, half // dims[3]), F32),
            pltpu.VMEM((n, n), BF16),
            pltpu.VMEM((n, n), BF16),
            pltpu.VMEM((n_row, n), F32),
            square, square, square, square, square, square, square, square,
            dma((n_row,)), dma((n_row,)),
            dma((2 * n_row,)), dma((2 * n_row,)),
            dma((2 * n_row,)), dma((2 * n_row,)),
            dma((16,)), dma((16,)), dma((1,)), dma((n_row,)),
            dma((8,)), dma((1,)), dma((4,)), dma((4,)), dma((2,)), dma((2,)), pltpu.SemaphoreType.REGULAR,
        ],
        compiler_params=pltpu.CompilerParams(
            collective_id=0, has_side_effects=True, vmem_limit_bytes=56 * 2**20
        ),
        name="exchange",
    )(order, mask, block)


def update_kernel(
    n_row, mask_smem, order_ref, mask_ref, r_ref, xh_ref, xl_ref, zh_ref, zl_ref, o_ref,
    r_high, r_low, slots_ref,
):
    a = pl.program_id(0)
    n = o_ref.shape[1]
    tile = n // 4
    r, c = lax.axis_index("row"), lax.axis_index("col")

    @pl.when(a == 0)
    def _():
        slots_ref[...] = arrival_slots(order_ref[pl.ds(r, 1), :], n_row, n // n_row)
        r_high[...], r_low[...] = split(r_ref[...])

    rows = pl.ds(pl.multiple_of(a * tile, tile), tile)
    place = one_hot(slots_ref[rows, :], n)
    o_ref[...] = jnp.zeros_like(o_ref)
    filled = [mask_smem[4 * r + a, 4 * c + q] for q in range(4)]
    seen = 0
    top = (r == 0) & (a < 2)
    for q in range(4):
        seen = seen + filled[q]
        for h in range(2):
            @pl.when((filled[q] == 1) & (seen == h + 1) & jnp.logical_not(top))
            def _():
                half = slice(tile * h, tile * h + tile)
                cols = slice(tile * q, tile * q + tile)
                value = bdot(place, r_high[:, half]) + bdot(place, r_low[:, half])
                panel = (xh_ref[rows, :], xl_ref[rows, :])
                o_ref[:, cols] = value - dot3(panel, (zh_ref[:, cols], zl_ref[:, cols]))

    @pl.when(c == 0)
    def _():
        mine = xh_ref[rows, :].astype(F32) + xl_ref[rows, :].astype(F32)
        above = iota(mine.shape, 1) > iota(mine.shape, 0) + a * tile
        o_ref[:, : 2 * tile] = jnp.where(above & top, 0.0, mine)


def update(order, mask, arrived, xh, xl, zh, zl):
    n_row, n = order.shape
    tile, pw = n // 4, n // 2

    def whole(shape):
        return pl.BlockSpec(shape, lambda a: (0,) * len(shape))

    def kernel(*refs):
        update_kernel(n_row, *refs)

    return pl.pallas_call(
        kernel,
        out_shape=jax.ShapeDtypeStruct((n, n), F32),
        grid=(4,),
        in_specs=[
            pl.BlockSpec(memory_space=pltpu.SMEM),
            whole(order.shape), whole(mask.shape),
            whole((n, pw)), whole((n, pw)), whole((n, pw)), whole((pw, n)), whole((pw, n)),
        ],
        out_specs=pl.BlockSpec((tile, n), lambda a: (a, 0)),
        scratch_shapes=[
            pltpu.VMEM((n, pw), BF16), pltpu.VMEM((n, pw), BF16), pltpu.VMEM((n, 128), jnp.int32),
        ],
        compiler_params=pltpu.CompilerParams(vmem_limit_bytes=48 * 2**20),
        name="update",
    )(mask, order, mask, arrived, xh, xl, zh, zl)


def on_device(assembled, row_order, tile_mask):
    n = assembled.shape[0]
    n_row, n_col = lax.axis_size("row"), lax.axis_size("col")
    order = row_order.reshape(n_row, n)
    arrived, xh, xl, zh, zl = exchange(order, tile_mask, assembled, n_row, n_col)
    return update(order, tile_mask, arrived.reshape(n, n // 2), xh, xl, zh, zl)


def solution(mesh):
    in_specs = (P("row", "col"), P(), P())
    out_specs = P("row", "col")
    return jax.shard_map(
        on_device, mesh=mesh, in_specs=in_specs, out_specs=out_specs, check_vma=False
    )
```

```python
import jax
import jax.numpy as jnp
from jax import lax
from jax.experimental import pallas as pl
from jax.experimental.pallas import tpu as pltpu
from jax.sharding import PartitionSpec as P

F32 = jnp.float32
BF16 = jnp.bfloat16
MESH = pl.DeviceIdType.MESH
NB = 128


def bdot(a, b, ca=1, cb=0):
    return lax.dot_general(a, b, (((ca,), (cb,)), ((), ())), preferred_element_type=F32)


def split(value):
    hi = value.astype(BF16)
    return hi, (value - hi.astype(F32)).astype(BF16)


def dot3(a, b, ca=1, cb=0):
    (ah, al), (bh, bl) = a, b
    return bdot(ah, bh, ca, cb) + (bdot(ah, bl, ca, cb) + bdot(al, bh, ca, cb))


def hdot(a, b, ca=1, cb=0):
    return lax.dot_general(
        a, b, (((ca,), (cb,)), ((), ())), precision=lax.Precision.HIGHEST, preferred_element_type=F32
    )


def iota(shape, dim):
    return lax.broadcasted_iota(jnp.int32, shape, dim)


def prefix_counts(flags):
    g, n = flags.shape
    parts = n // 128
    flags = flags.astype(BF16)
    stacked = jnp.concatenate([flags[:, 128 * i : 128 * i + 128] for i in range(parts)], axis=0)
    before = (iota((128, 128), 0) < iota((128, 128), 1)).astype(F32).astype(BF16)
    inner = bdot(stacked, before)
    totals = jnp.sum(stacked.astype(F32), axis=1, keepdims=True)
    out = []
    offset = jnp.zeros((g, 1), F32)
    for i in range(parts):
        out.append(inner[g * i : g * i + g] + offset)
        offset = offset + totals[g * i : g * i + g]
    return jnp.concatenate(out, axis=1)


def arrival_slots(order_row, n_row, share):
    n = order_row.shape[1]
    source = order_row // n
    flags = (jnp.broadcast_to(source, (n_row, n)) == iota((n_row, n), 0)).astype(F32)
    rank = jnp.sum(flags * prefix_counts(flags), axis=0, keepdims=True)
    slot = source.astype(F32) * share + rank
    return jnp.transpose(jnp.broadcast_to(slot, (128, n))).astype(jnp.int32)


def one_hot(slots, n):
    return (slots[:, 0:1] == iota((slots.shape[0], n), 1)).astype(F32).astype(BF16)


def selections(mask, group):
    tiles = mask.shape[1]
    at, lane = iota((tiles, 128), 0), iota((tiles, 128), 1)
    start = 4 * group
    here = (at == start + lane % 4) & (lane < 8)
    upto = (at >= start) & (at <= start + lane % 4) & (lane < 8)
    mask = mask.astype(F32).astype(BF16)
    filled = bdot(mask, here.astype(F32).astype(BF16))
    count = bdot(mask, upto.astype(F32).astype(BF16))
    return filled * (count == (1 + lane[:1] // 4).astype(F32)).astype(F32)


def expand_tile(pair, first, second):
    half = pair.shape[1] // 2
    return first * pair[:, :half] + second * pair[:, half:]


def reciprocal(d):
    guess = pltpu.reciprocal(d, approx=True)
    return guess * (2.0 - d * guess)


def tree_sum(terms):
    while len(terms) > 1:
        terms = [terms[i] + terms[i + 1] for i in range(0, len(terms), 2)]
    return terms[0]


def inverse_factor_block(block):
    n = block.shape[0]
    groups = n // 8
    rows = [block[8 * g : 8 * g + 8, :] for g in range(groups)]
    lane = iota((8, n), 1)
    sub = iota((8, n), 0)
    other = [jnp.where(lane == sub + 8 * g, 1.0, 0.0) for g in range(groups)]
    out = []
    for g0 in range(groups):
        lead = rows[g0]
        c0 = 8 * g0

        def replicated(i, j):
            column = jnp.broadcast_to(lead[:, c0 + j : c0 + j + 1], (8, n))
            return jnp.broadcast_to(column[i : i + 1, :], (8, n))

        a = [[replicated(i, j) for j in range(i + 1)] for i in range(8)]
        m = [[None] * 8 for _ in range(8)]
        inv = []
        for k in range(8):
            inv.append(reciprocal(a[k][k]))
            for i in range(k + 1, 8):
                ratio = a[i][k] * inv[k]
                for j in range(k + 1, i + 1):
                    a[i][j] = a[i][j] - ratio * a[j][k]
                for j in range(k):
                    m[i][j] = m[i][j] - ratio * m[k][j]
                m[i][k] = -ratio

        def lower(v):
            res = []
            for i in range(8):
                total = v[i]
                for j in range(i):
                    total = total + m[i][j] * v[j]
                res.append(total)
            return res

        def upper(v):
            v = [v[i] * inv[i] for i in range(8)]
            res = []
            for j in range(8):
                total = v[j]
                for i in range(j + 1, 8):
                    total = total + m[i][j] * v[i]
                res.append(total)
            return res

        own = lower([jnp.broadcast_to(other[g0][i : i + 1, :], (8, n)) for i in range(8)])
        done = own[0] * lax.rsqrt(a[0][0])
        for i in range(1, 8):
            done = jnp.where(sub == i, own[i] * lax.rsqrt(a[i][i]), done)
        out.append(done)
        if g0 == groups - 1:
            break
        t = upper(lower([jnp.broadcast_to(lead[i : i + 1, :], (8, n)) for i in range(8)]))
        u = upper(own)
        for g in range(g0 + 1, groups):
            c = [jnp.broadcast_to(rows[g][:, c0 + j : c0 + j + 1], (8, n)) for j in range(8)]
            rows[g] = rows[g] - tree_sum([c[j] * t[j] for j in range(8)])
            other[g] = other[g] - tree_sum([c[j] * u[j] for j in range(8)])
    return jnp.concatenate(out, axis=0)


def factor_blocks(s_ref, a_ref, o_ref, done):
    n = s_ref.shape[0]
    a_ref[...] = s_ref[...]
    o_ref[...] = (iota((n, n), 0) == iota((n, n), 1)).astype(F32)

    def step(b, carry):
        start = pl.multiple_of(b * NB, NB)
        block = pl.ds(start, NB)
        inverse = inverse_factor_block(a_ref[block, block])
        mine = dot3(split(inverse), split(o_ref[block, :]))
        done(b, mine)

        @pl.when(b < n // NB - 1)
        def _():
            below = hdot(a_ref[:, block], inverse, 1, 1)
            below = jnp.where(iota((n, NB), 0) >= start + NB, below, 0.0)
            a_ref[...] = a_ref[...] - hdot(below, below, 1, 1)
            o_ref[...] = o_ref[...] - dot3(split(below), split(mine))

        return carry

    lax.fori_loop(0, n // NB, step, 0)


def exchange_kernel(
    dims, order_ref, mask_ref, x_ref, r_ref, xh_out, xl_out, zh_out, zl_out,
    packed, lead, strip, high, low, rank_ref, top_ref, tr_ref, s_ref, a_ref, o_ref, inv_ref,
    unpack_ref, th_ref, tl_ref, rh_ref, rl_ref, xh_ref, xl_ref, zh_ref, zl_ref,
    a2a_send, a2a_recv, z_send, z_recv, y_send, y_recv, strip_send, strip_recv, row_send, row_recv,
    fill_send, fill_recv, tr_send, tr_recv, inv_send, inv_recv, local, go,
):
    ny, nz, nzl, nx = dims
    n_row, share, half = packed.shape
    n = x_ref.shape[0]
    tile = half // 2
    pw = top_ref.shape[0]
    r = lax.axis_index("row")
    c = lax.axis_index("col")
    n_col = lax.axis_size("col")
    y, z = r // nz, r % nz
    plane = 2 * nx
    zl, x, core = c // plane, (c // 2) % nx, c % 2
    width = half // nx
    mirror = (c == r) & (core == 1)

    barrier = pltpu.get_barrier_semaphore()
    for k in range(1, n_row):
        pl.semaphore_signal(barrier, inc=1, device_id=((r + k) % n_row, c), device_id_type=MESH)
    for k in range(1, n_col):
        pl.semaphore_signal(barrier, inc=1, device_id=(r, (c + k) % n_col), device_id_type=MESH)

    @pl.when(core == 1)
    def _():
        for k in range(n_row):
            @pl.when((c != r) | (k != 0))
            def _():
                pl.semaphore_signal(barrier, inc=1, device_id=((r + k) % n_row, r), device_id_type=MESH)

    match = order_ref[...] // n == r
    rank_ref[...] = jnp.where(match, prefix_counts(match.astype(F32)), -1.0)
    code_row = (order_ref[...] % n + n * (iota((n_row, n), 1) // tile)).astype(F32)
    sel = selections(mask_ref[...], c)
    high[...], low[...] = split(x_ref[...])

    def pack(first, last):
        cols = []
        for t in range(first, last):
            hit = jnp.broadcast_to(rank_ref[t : t + 1, :], (share, n)) == iota((share, n), 0).astype(F32)
            code = jnp.where(hit, jnp.broadcast_to(code_row[t : t + 1, :], (share, n)), 0.0)
            cols.append(jnp.sum(code, axis=1, keepdims=True) + float(4 * n * t))
        code = jnp.concatenate(cols, axis=0).astype(jnp.int32)
        rows = (last - first) * share
        pick = (code % n == iota((rows, n), 1)).astype(F32).astype(BF16)
        tile_row = (code // n == iota((rows, 4 * n_row), 1)).astype(F32).astype(BF16)
        weights = bdot(tile_row, sel.astype(BF16))
        got = bdot(pick, high[...]) + bdot(pick, low[...])
        for h in range(2):
            total = jnp.zeros((rows, tile), F32)
            for q in range(4):
                w = weights[:, 4 * h + q : 4 * h + q + 1]
                total = total + w * got[:, tile * q : tile * q + tile]
            for i in range(last - first):
                packed[first + i, :, tile * h : tile * h + tile] = total[share * i : share * i + share]

    pack(0, 4)
    lead[r] = packed[0]
    greeted = n_row - 1 + n_col - 1 + nzl * nx
    pl.when(mirror)(lambda: pl.semaphore_wait(barrier, greeted - 1))
    pl.when(jnp.logical_not(mirror))(lambda: pl.semaphore_wait(barrier, greeted))

    class Gather:
        def __init__(self, ref, base):
            self.ref, self.base = ref, base

        def copy(self, slot, sends, recvs, sem, row):
            slot = self.ref.at[slot]
            return pltpu.make_async_remote_copy(
                slot, slot, sends.at[self.base + sem], recvs.at[self.base + sem],
                device_id=(row, c), device_id_type=MESH)

        def z_copy(self, k):
            return self.copy(r, z_send, z_recv, k, y * nz + (z + k) % nz)

        def z_arrival(self, k):
            return self.copy(y * nz + (z - k + nz) % nz, z_send, z_recv, k, r)

        def y_copy(self, k, d):
            return self.copy(y * nz + (z - k + nz) % nz, y_send, y_recv, k * ny + d, ((y + d) % ny) * nz + z)

        def y_arrival(self, k, d):
            return self.copy(
                ((y - d + ny) % ny) * nz + (z - k + nz) % nz, y_send, y_recv, k * ny + d, r)

        def start_z(self):
            for k in range(1, nz):
                self.z_copy(k).start()

        def start_y(self):
            for d in range(1, ny):
                self.y_copy(0, d).start()

        def forward(self):
            for k in range(1, nz):
                self.z_arrival(k).wait_recv()
                for d in range(1, ny):
                    self.y_copy(k, d).start()

        def receive(self):
            for k in range(nz):
                for d in range(1, ny):
                    self.y_arrival(k, d).wait_recv()

        def finish(self):
            for k in range(1, nz):
                self.z_copy(k).wait_send()
            for k in range(nz):
                for d in range(1, ny):
                    self.y_copy(k, d).wait_send()

    own_lead = Gather(lead, 0)
    top_strip = Gather(strip, n_row)

    def scatter_copy(p, q):
        return pltpu.make_async_remote_copy(
            packed.at[0, :, pl.ds(q * width, width)], strip.at[r], strip_send.at[p * nx + q], strip_recv.at[0],
            device_id=(r, p * plane + 2 * q), device_id_type=MESH)

    def row_copy(p, q):
        return pltpu.make_async_remote_copy(
            packed.at[0, :, pl.ds(q * width, width)], strip.at[r], row_send.at[p * nx + q], row_recv.at[r],
            device_id=(c, p * plane + 2 * q + 1), device_id_type=MESH)

    def row_arrival(k):
        return pltpu.make_async_remote_copy(
            strip.at[k], strip.at[k], row_send.at[0], row_recv.at[k], device_id=(r, c), device_id_type=MESH)

    def each_row_copy(do):
        for p in range(nzl):
            for q in range(nx):
                @pl.when((c != r) | (c != p * plane + 2 * q + 1))
                def _():
                    do(row_copy(p, q))

    def strip_columns(at):
        return top_ref.at[:, pl.ds(pl.multiple_of(at * width, width), width)]

    def fill_copy(dx):
        return pltpu.make_async_remote_copy(
            strip_columns(x), strip_columns(x), fill_send.at[dx], fill_recv.at[dx],
            device_id=(r, zl * plane + 2 * ((x + dx) % nx) + core), device_id_type=MESH)

    def fill_arrival(dx):
        cols = strip_columns((x - dx + nx) % nx)
        return pltpu.make_async_remote_copy(
            cols, cols, fill_send.at[dx], fill_recv.at[dx], device_id=(r, c), device_id_type=MESH)

    def tr_copy():
        return pltpu.make_async_remote_copy(
            top_ref, tr_ref, tr_send.at[0], tr_recv.at[0],
            device_id=(r, c + 1 - 2 * core), device_id_type=MESH)

    def inverse_copy(part):
        rows = pl.ds(0, pw - NB) if part == 0 else pl.ds(pw - NB, NB)
        return pltpu.make_async_remote_copy(
            inv_ref.at[rows], inv_ref.at[rows], inv_send.at[part], inv_recv.at[part],
            device_id=(r, c + 1 - 2 * core), device_id_type=MESH)

    offsets = [(dy, dz) for dy in range(ny) for dz in range(nz) if dy + dz > 0]

    def a2a_copy(dy, dz):
        target = ((y + dy) % ny) * nz + (z + dz) % nz
        return target, pltpu.make_async_remote_copy(
            packed.at[target], r_ref.at[r], a2a_send.at[dy * nz + dz], a2a_recv.at[dy * nz + dz],
            device_id=(target, c), device_id_type=MESH)

    def a2a_arrival(dy, dz):
        slot = r_ref.at[((y - dy + ny) % ny) * nz + (z - dz + nz) % nz]
        return pltpu.make_async_remote_copy(
            slot, slot, a2a_send.at[dy * nz + dz], a2a_recv.at[dy * nz + dz], device_id=(r, c), device_id_type=MESH)

    def start_a2a(dy):
        for dz in range(nz):
            if dy + dz > 0:
                target, copy = a2a_copy(dy, dz)
                pl.when(target != 0)(copy.start)

    @pl.when(c == 0)
    def _():
        for p in reversed(range(nzl)):
            for q in range(nx):
                if p + q > 0:
                    scatter_copy(p, q).start()
        strip[r] = packed[0, :, 0:width]

    @pl.when(core == 0)
    def _():
        @pl.when(c != 0)
        def _():
            scatter_copy(0, 1).wait_recv()
        top_strip.start_z()
        top_strip.start_y()

    @pl.when(mirror)
    def _():
        for q in range(nx):
            @pl.when(x == q)
            def _():
                strip[r] = packed[0, :, q * width : q * width + width]

    pack(4, n_row)

    @pl.when(core == 0)
    def _():
        top_strip.forward()
        pl.semaphore_signal(go, inc=1, device_id=(r, c + 1), device_id_type=MESH)
        own_lead.start_z()

    @pl.when(core == 1)
    def _():
        pl.semaphore_wait(go, 1)
        own_lead.start_z()

    each_row_copy(lambda copy: copy.start())
    own_lead.start_y()
    unpack_ref[...] = one_hot(arrival_slots(order_ref[0:1, :], n_row, share)[:pw], n)

    def keep_copy():
        return pltpu.make_async_copy(packed.at[r], r_ref.at[r], local.at[4])

    pl.when(r != 0)(lambda: keep_copy().start())

    def in_order(ref, cols):
        unpack = unpack_ref[...]
        first, second = split(ref[...].reshape(n_row * share, cols))
        return bdot(unpack, first) + bdot(unpack, second)

    def dense(pairs, marks):
        rows = []
        for i in range(2):
            pair = pairs[tile * i : tile * i + tile, :]
            rows.append(jnp.concatenate([
                expand_tile(pair, marks[i : i + 1, q : q + 1], marks[i : i + 1, 4 + q : 5 + q])
                for q in range(4)], axis=1))
        return jnp.concatenate(rows, axis=0)

    def lead_copy():
        return pltpu.make_async_copy(lead, r_ref, local.at[4])

    def own_top():
        own_lead.receive()
        pl.when(r == 0)(lambda: lead_copy().start())
        th_ref[...], tl_ref[...] = split(dense(in_order(lead, half), sel))

    def own_rows(ref):
        rh_ref[...], rl_ref[...] = split(jnp.transpose(dense(ref[...], selections(mask_ref[...], r))))

    def start_fill():
        top_ref[:, pl.ds(pl.multiple_of(x * width, width), width)] = in_order(strip, width)
        for dx in range(1, nx):
            fill_copy(dx).start()

    def start_rest():
        for dy in range(ny):
            start_a2a(dy)
        own_lead.forward()

    @pl.when(core == 0)
    def _():
        top_strip.receive()
        start_fill()
        start_rest()
        for dx in range(1, nx):
            fill_arrival(dx).wait_recv()
        marks = selections(mask_ref[...], 0)
        for a in range(2):
            pair = top_ref[tile * a : tile * a + tile, :]
            for q in range(2):
                s_ref[tile * a : tile * a + tile, tile * q : tile * q + tile] = expand_tile(
                    pair, marks[a : a + 1, q : q + 1], marks[a : a + 1, 4 + q : 5 + q])

        def beside():
            own_top()
            tr_copy().wait_recv()
            own_rows(tr_ref)

        def done(b, rows):
            inv_ref[pl.ds(pl.multiple_of(b * NB, NB), NB), :] = rows
            for part in range(2):
                pl.when(b == pw // NB - 2 + part)(inverse_copy(part).start)

        factor_blocks(s_ref, a_ref, o_ref, done)
        beside()

    @pl.when(core == 1)
    def _():
        start_rest()
        for k in range(n_row):
            @pl.when((c != r) | (r != k))
            def _():
                row_arrival(k).wait_recv()
        start_fill()
        for dx in range(1, nx):
            fill_arrival(dx).wait_recv()
        tr_copy().start()
        own_rows(top_ref)
        own_top()
        for part in range(2):
            inverse_copy(part).wait_recv()

    inverse = split(inv_ref[...])
    zh_ref[...], zl_ref[...] = split(dot3(inverse, (th_ref[...], tl_ref[...])))
    xh_ref[...], xl_ref[...] = split(dot3((rh_ref[...], rl_ref[...]), inverse, 1, 1))
    outs = [
        pltpu.make_async_copy(a, b, local.at[i])
        for i, (a, b) in enumerate([(xh_ref, xh_out), (xl_ref, xl_out), (zh_ref, zh_out), (zl_ref, zl_out)])
    ]
    for copy in outs:
        copy.start()

    own_lead.finish()
    each_row_copy(lambda copy: copy.wait_send())

    @pl.when(c == 0)
    def _():
        for p in range(nzl):
            for q in range(nx):
                if p + q > 0:
                    scatter_copy(p, q).wait_send()

    for dx in range(1, nx):
        fill_copy(dx).wait_send()

    @pl.when(core == 0)
    def _():
        top_strip.finish()
        for part in range(2):
            inverse_copy(part).wait_send()

    pl.when(core == 1)(lambda: tr_copy().wait_send())
    for dy, dz in offsets:
        target, copy = a2a_copy(dy, dz)
        pl.when(target != 0)(copy.wait_send)
    for copy in outs:
        copy.wait()

    @pl.when(r != 0)
    def _():
        keep_copy().wait()
        for dy, dz in offsets:
            a2a_arrival(dy, dz).wait_recv()

    pl.when(r == 0)(lambda: lead_copy().wait())


def exchange(order, mask, block, n_row, n_col):
    n = block.shape[0]
    share, half, pw = n // n_row, n // 2, n // 2
    dims = (n_row // 4, 4, 2, n_col // 4)
    vmem = pl.BlockSpec(memory_space=pltpu.VMEM)
    dma = pltpu.SemaphoreType.DMA
    square = pltpu.VMEM((pw, pw), F32)
    wide, tall = pltpu.VMEM((pw, n), BF16), pltpu.VMEM((n, pw), BF16)

    def kernel(*refs):
        exchange_kernel(dims, *refs)

    return pl.pallas_call(
        kernel,
        out_shape=[
            jax.ShapeDtypeStruct((n_row, share, half), F32),
            jax.ShapeDtypeStruct((n, pw), BF16),
            jax.ShapeDtypeStruct((n, pw), BF16),
            jax.ShapeDtypeStruct((pw, n), BF16),
            jax.ShapeDtypeStruct((pw, n), BF16),
        ],
        in_specs=[vmem] * 3,
        out_specs=[pl.BlockSpec(memory_space=pl.ANY)] * 5,
        scratch_shapes=[
            pltpu.VMEM((n_row, share, half), F32),
            pltpu.VMEM((n_row, share, half), F32),
            pltpu.VMEM((n_row, share, half // dims[3]), F32),
            pltpu.VMEM((n, n), BF16),
            pltpu.VMEM((n, n), BF16),
            pltpu.VMEM((n_row, n), F32),
            square, square, square, square, square, square,
            wide, wide, wide, tall, tall, tall, tall, wide, wide,
            dma((n_row,)), dma((n_row,)),
            dma((2 * n_row,)), dma((2 * n_row,)),
            dma((2 * n_row,)), dma((2 * n_row,)),
            dma((8,)), dma((1,)), dma((8,)), dma((n_row,)),
            dma((4,)), dma((4,)), dma((1,)), dma((1,)), dma((2,)), dma((2,)),
            dma((5,)), pltpu.SemaphoreType.REGULAR,
        ],
        compiler_params=pltpu.CompilerParams(
            collective_id=0, has_side_effects=True, vmem_limit_bytes=56 * 2**20
        ),
        name="exchange",
    )(order, mask, block)


def update_kernel(
    n_row, mask_smem, order_ref, mask_ref, r_ref, xh_ref, xl_ref, zh_ref, zl_ref, o_ref,
    r_high, r_low, slots_ref,
):
    a = pl.program_id(0)
    n = o_ref.shape[1]
    tile = n // 4
    r, c = lax.axis_index("row"), lax.axis_index("col")

    @pl.when(a == 0)
    def _():
        slots_ref[...] = arrival_slots(order_ref[pl.ds(r, 1), :], n_row, n // n_row)
        r_high[...], r_low[...] = split(r_ref[...])

    rows = pl.ds(pl.multiple_of(a * tile, tile), tile)
    place = one_hot(slots_ref[rows, :], n)
    o_ref[...] = jnp.zeros_like(o_ref)
    filled = [mask_smem[4 * r + a, 4 * c + q] for q in range(4)]
    seen = 0
    top = (r == 0) & (a < 2)
    for q in range(4):
        seen = seen + filled[q]
        for h in range(2):
            @pl.when((filled[q] == 1) & (seen == h + 1) & jnp.logical_not(top))
            def _():
                half = slice(tile * h, tile * h + tile)
                cols = slice(tile * q, tile * q + tile)
                value = bdot(place, r_high[:, half]) + bdot(place, r_low[:, half])
                panel = (xh_ref[rows, :], xl_ref[rows, :])
                o_ref[:, cols] = value - dot3(panel, (zh_ref[:, cols], zl_ref[:, cols]))

    @pl.when(c == 0)
    def _():
        mine = xh_ref[rows, :].astype(F32) + xl_ref[rows, :].astype(F32)
        above = iota(mine.shape, 1) > iota(mine.shape, 0) + a * tile
        o_ref[:, : 2 * tile] = jnp.where(above & top, 0.0, mine)


def update(order, mask, arrived, xh, xl, zh, zl):
    n_row, n = order.shape
    tile, pw = n // 4, n // 2

    def whole(shape):
        return pl.BlockSpec(shape, lambda a: (0,) * len(shape))

    def kernel(*refs):
        update_kernel(n_row, *refs)

    return pl.pallas_call(
        kernel,
        out_shape=jax.ShapeDtypeStruct((n, n), F32),
        grid=(4,),
        in_specs=[
            pl.BlockSpec(memory_space=pltpu.SMEM),
            whole(order.shape), whole(mask.shape),
            whole((n, pw)), whole((n, pw)), whole((n, pw)), whole((pw, n)), whole((pw, n)),
        ],
        out_specs=pl.BlockSpec((tile, n), lambda a: (a, 0)),
        scratch_shapes=[
            pltpu.VMEM((n, pw), BF16), pltpu.VMEM((n, pw), BF16), pltpu.VMEM((n, 128), jnp.int32),
        ],
        compiler_params=pltpu.CompilerParams(vmem_limit_bytes=60 * 2**20),
        name="update",
    )(mask, order, mask, arrived, xh, xl, zh, zl)


def on_device(assembled, row_order, tile_mask):
    n = assembled.shape[0]
    n_row, n_col = lax.axis_size("row"), lax.axis_size("col")
    order = row_order.reshape(n_row, n)
    arrived, xh, xl, zh, zl = exchange(order, tile_mask, assembled, n_row, n_col)
    return update(order, tile_mask, arrived.reshape(n, n // 2), xh, xl, zh, zl)


def solution(mesh):
    in_specs = (P("row", "col"), P(), P())
    out_specs = P("row", "col")
    return jax.shard_map(
        on_device, mesh=mesh, in_specs=in_specs, out_specs=out_specs, check_vma=False
    )
```
